32 devices in a mesh: req: 8 (over z, x), mlp: 4 (over y, core).
Axes of the slice: x: 2, y: 2, z: 4, core: 2. Of those that a mesh axis runs over, the one named last changes fastest.
Arguments:
- patches: bfloat16 [7680, 4096], P('req'), may hold values from -6 to 6
- norm_gain: float32 [4096], replicated, may hold values from 0.25 to 1.75
- norm_bias: float32 [4096], replicated, may hold values from -3 to 3
- gate_weight: bfloat16 [4096, 8192], P(None, ('req', 'mlp')), may hold values from -0.09375 to 0.09375
- up_weight: bfloat16 [4096, 8192], P(None, ('req', 'mlp')), may hold values from -0.09375 to 0.09375
- down_weight: bfloat16 [4096, 8192], P(None, ('req', 'mlp')), may hold values from -0.0625 to 0.0625
- layer_scale: float32 [4096], replicated, may hold values from 0.25 to 2.5
- projection: bfloat16 [4, 4096, 4096], P(None, 'mlp', 'req'), may hold values from -0.046875 to 0.046875
- text_rows: bfloat16 [32768, 4096], P(('req', 'mlp')), may hold values from -6 to 6
- destination: int32 [1920], replicated, may hold values from -1 to 32767, as said below
Outputs:
- patch_out: bfloat16 [7680, 4096], P('req', 'mlp')
- streams: bfloat16 [32768, 4096], P(('req', 'mlp'))
The draws below stay inside these ranges and needn't reach their ends.
Inputs may be any that keep to these rules, and one draw needn't show every extreme that they name: `destination`: values other than -1 are distinct positions; the positions landing in one piece of 1024 consecutive positions (a stream holds 4 pieces) form one run of consecutive positions, at least one and at most 60 of them, and some piece receives exactly 60.
All inputs are finite; a program needn't handle non-finite values.
Results may differ from the reference program's by a relative error of at most 0.015.
Values may be sent and summed in bfloat16 or wider, within the bound.
A program may use at most 128 MiB of HBM per device.

```python
import math
import jax
import jax.numpy as jnp
from jax import lax

D = 4096
FF = 8192
DOUT = 4096
L = 4096
PATCHES = 7680
SLOTS = 1920
NS = 8
PIECE = 1024
CAP = 60
N_REQ = 8
N_MLP = 4


def draw_destination(key, part):
    cells = NS * N_MLP
    key_count, key_top, key_start, key_order = jax.random.split(jax.random.fold_in(key, 17), 4)
    counts = jax.random.randint(key_count, (cells,), (CAP + 1) // 2, CAP + 1)
    chosen = jax.random.randint(key_top, (), 0, cells)
    cell_ids = jnp.arange(cells)
    counts = jnp.where(cell_ids == (chosen + 1) % cells, (CAP + 1) // 2, counts)
    counts = jnp.where(cell_ids == chosen, CAP, counts)
    starts = jax.random.randint(key_start, (cells,), 0, PIECE - counts + 1)
    starts = jnp.where(cell_ids == cells - 1, PIECE - counts, starts)
    row_index = jnp.arange(cells * CAP)
    cell_of = row_index // CAP
    rank_of = row_index % CAP
    values = jnp.where(rank_of < counts[cell_of], cell_of * PIECE + starts[cell_of] + rank_of, -1)
    order = jax.random.permutation(key_order, cells * CAP)
    return jnp.zeros((cells * CAP,), jnp.int32).at[order].set(values.astype(jnp.int32))


def shard_levels(stream_key, shape, cuts, least, top_value):
    def one(position, blocks):
        heights = jax.random.uniform(jax.random.fold_in(jax.random.fold_in(stream_key, 6), position), (blocks,), jnp.float32, least / len(cuts), top_value / len(cuts))
        return jnp.repeat(jnp.exp(heights), shape[position] // blocks).reshape((-1,) + (1,) * (len(shape) - position - 1))

    loudness = one(*cuts[0])
    for cut in cuts[1:]:
        loudness = loudness * one(*cut)
    return loudness


def bell_draw(stream_key, dims, width, reach, shards=(), held_as=jnp.bfloat16):
    result = width * jax.random.normal(stream_key, dims, jnp.float32)
    if shards:
        result = result * shard_levels(stream_key, dims, shards, -0.22, 0.18)
    return jnp.clip(result, -reach, reach).astype(held_as)


def setup_inputs(seed: int = 0) -> dict:
    key_list = jax.random.split(jax.random.key(seed), 11)
    return {
        "patches": bell_draw(key_list[0], (PATCHES, D), 1.0, 6.0, ((0, 8),)),
        "norm_gain": jnp.clip(1.0 + 0.15 * jax.random.normal(key_list[1], (D,), jnp.float32), 0.25, 1.75),
        "norm_bias": bell_draw(key_list[2], (D,), 0.5, 3.0, (), jnp.float32),
        "gate_weight": bell_draw(key_list[3], (D, FF), D ** -0.5, 0.09375, ((1, 32),)),
        "up_weight": bell_draw(key_list[4], (D, FF), D ** -0.5, 0.09375, ((1, 32),)),
        "down_weight": bell_draw(key_list[5], (D, FF), FF ** -0.5, 0.0625, ((1, 32),)),
        "layer_scale": jnp.clip(jnp.exp(jax.random.uniform(key_list[6], (D,), jnp.float32, math.log(0.25), math.log(2.5))), 0.25, 2.5),
        "projection": bell_draw(key_list[7], (4, D, DOUT), (4 * D) ** -0.5, 0.046875, ((1, 4), (2, 8))),
        "text_rows": bell_draw(key_list[8], (NS * L, DOUT), 1.0, 6.0, ((0, 32),)),
        "destination": draw_destination(jax.random.fold_in(key_list[10], 71), 0),
    }


def layer_norm(values, norm_gain, norm_bias):
    row_mean = lax.optimization_barrier(jnp.mean(values, axis=-1, keepdims=True))
    centred = values - row_mean
    variance = lax.optimization_barrier(jnp.mean(centred * centred, axis=-1, keepdims=True))
    return centred * lax.rsqrt(variance + 1e-06) * norm_gain + norm_bias

def reference(patches, norm_gain, norm_bias, gate_weight, up_weight, down_weight, layer_scale, projection, text_rows, destination):
    model_width = patches.shape[1]
    unit_block = FF // (N_REQ * N_MLP)
    inputs = patches.astype(jnp.float32)
    normed = layer_norm(inputs, norm_gain, norm_bias).astype(jnp.bfloat16)
    gate_grouped = gate_weight.reshape(model_width, N_REQ, N_MLP, unit_block)
    up_grouped = up_weight.reshape(model_width, N_REQ, N_MLP, unit_block)
    down_grouped = down_weight.reshape(model_width, N_REQ, N_MLP, unit_block)
    ffn_total = jnp.zeros(inputs.shape, jnp.float32)
    for group_index in range(N_MLP):
        gate_cols = gate_grouped[:, :, group_index, :].reshape(model_width, N_REQ * unit_block)
        up_cols = up_grouped[:, :, group_index, :].reshape(model_width, N_REQ * unit_block)
        down_cols = down_grouped[:, :, group_index, :].reshape(model_width, N_REQ * unit_block)
        gate_act = jnp.dot(normed, gate_cols, preferred_element_type=jnp.float32)
        up_act = jnp.dot(normed, up_cols, preferred_element_type=jnp.float32)
        hidden = (jax.nn.silu(gate_act) * up_act).astype(jnp.bfloat16)
        partial_value = jnp.dot(hidden, down_cols.T, preferred_element_type=jnp.float32).astype(jnp.bfloat16)
        ffn_total = ffn_total + lax.optimization_barrier(partial_value).astype(jnp.float32)
    patch_out = (inputs + layer_scale * ffn_total).astype(jnp.bfloat16)
    merged = patch_out.reshape(SLOTS, 4, model_width)
    projected = jnp.zeros((SLOTS, DOUT), jnp.float32)
    for quarter in range(4):
        projected = projected + jnp.dot(merged[:, quarter, :], projection[quarter], preferred_element_type=jnp.float32)
    projected = projected.astype(jnp.bfloat16)
    target = jnp.where(destination >= 0, destination, NS * L).astype(jnp.int32)
    streams = text_rows.at[target].set(projected, mode='drop')
    return (patch_out, streams)
```

```python
import jax
import jax.numpy as jnp
from jax import lax
from jax.sharding import PartitionSpec as P


def layer_norm(values, norm_gain, norm_bias):
    row_mean = jnp.mean(values, axis=-1, keepdims=True)
    centred = values - row_mean
    variance = jnp.mean(centred * centred, axis=-1, keepdims=True)
    return centred * lax.rsqrt(variance + 1e-06) * norm_gain + norm_bias


def shards(
    patches,
    norm_gain,
    norm_bias,
    gate_weight,
    up_weight,
    down_weight,
    layer_scale,
    projection,
    text_rows,
    destination,
):
    req_count = lax.axis_size("req")
    mlp_count = lax.axis_size("mlp")
    req_index = lax.axis_index("req")
    mlp_index = lax.axis_index("mlp")
    far_count = 4
    near_count = req_count // far_count
    pair_count = mlp_count // 2
    far, near = req_index // near_count, req_index % near_count
    pair, core = mlp_index // 2, mlp_index % 2

    def shift_far(x, s):
        perm = [
            (f * near_count + n, ((f + s) % far_count) * near_count + n)
            for f in range(far_count)
            for n in range(near_count)
        ]
        return lax.ppermute(x, "req", perm)

    def shift_near(x, s):
        perm = [
            (f * near_count + n, f * near_count + (n + s) % near_count)
            for f in range(far_count)
            for n in range(near_count)
        ]
        return lax.ppermute(x, "req", perm)

    def shift_pair(x, s):
        perm = [(p * 2 + c, ((p + s) % pair_count) * 2 + c) for p in range(pair_count) for c in range(2)]
        return lax.ppermute(x, "mlp", perm)

    def swap_core(x):
        return lax.ppermute(x, "mlp", [(m, m ^ 1) for m in range(mlp_count)])

    rows_here, model_width = patches.shape
    feat_width = model_width // mlp_count

    def with_near(w):
        return jnp.concatenate([w] + [shift_near(w, s) for s in range(1, near_count)], axis=1)

    def quarter_at(t, d, sign):
        other = (pair + sign * t) % pair_count
        return (other * 2 + (core + d) % 2) * feat_width

    def relative(x, axis, sign, which):
        return jnp.concatenate(
            [lax.dynamic_slice_in_dim(x, quarter_at(t, d, sign), feat_width, axis=axis) for t, d in which], axis=axis
        )

    both = [(t, d) for d in range(2) for t in range(pair_count)]
    kept = [(t, 0) for t in range(pair_count)]
    sent = [(t, 1) for t in range(pair_count)]

    inputs = patches.astype(jnp.float32)
    normed = layer_norm(inputs, norm_gain, norm_bias).astype(jnp.bfloat16)
    own_quarter = lax.dynamic_slice_in_dim(normed, mlp_index * feat_width, feat_width, axis=1)
    gate_full = with_near(gate_weight)
    up_full = with_near(up_weight)
    down_full = with_near(down_weight)
    gate_rel = relative(gate_full, 0, -1, both)
    up_rel = relative(up_full, 0, -1, both)
    down_sent = relative(down_full, 0, 1, sent)
    down_kept = relative(down_full, 0, 1, kept)

    def normed_block(s):
        if s == 0:
            return relative(normed, 1, -1, both)
        first = shift_far(own_quarter, s)
        column = [first] + [shift_pair(first, t) for t in range(1, pair_count)]
        return jnp.concatenate(column + [swap_core(c) for c in column], axis=1)

    blocks = [normed_block(s) for s in range(far_count)]

    def dot_t(a, w):
        return lax.dot_general(a, w, (((1,), (1,)), ((), ())), preferred_element_type=jnp.float32)

    total = None
    for s in (1, 3, 2, 0):
        block = blocks[s]
        gate_act = jnp.dot(block, gate_rel, preferred_element_type=jnp.float32)
        up_act = jnp.dot(block, up_rel, preferred_element_type=jnp.float32)
        hidden = (jax.nn.silu(gate_act) * up_act).astype(jnp.bfloat16)
        from_core = swap_core(dot_t(hidden, down_sent).astype(jnp.bfloat16))
        of_core = dot_t(hidden, down_kept) + from_core.astype(jnp.float32)
        mine = of_core[:, :feat_width]
        for t in range(1, pair_count):
            part = of_core[:, t * feat_width : (t + 1) * feat_width].astype(jnp.bfloat16)
            mine = mine + shift_pair(part, t).astype(jnp.float32)
        if s:
            mine = shift_far(mine.astype(jnp.bfloat16), far_count - s).astype(jnp.float32)
        total = mine if total is None else total + mine

    scale_here = lax.dynamic_slice_in_dim(layer_scale, mlp_index * feat_width, feat_width)
    own_inputs = lax.dynamic_slice_in_dim(patches, mlp_index * feat_width, feat_width, axis=1).astype(jnp.float32)
    patch_out = (own_inputs + scale_here * total).astype(jnp.bfloat16)

    merged = patch_out.reshape(rows_here // 4, 4 * feat_width)
    weight_cols = projection.reshape(4 * feat_width, projection.shape[2])
    slots_here = rows_here // 4
    piece_rows = text_rows.shape[0]
    slot_count = destination.shape[0]
    bucket_count = req_count * mlp_count
    capacity = slot_count // bucket_count
    is_valid = destination >= 0
    piece_ids = jnp.where(is_valid, destination // piece_rows, -1)
    offsets = destination % piece_rows
    bucket_hit = piece_ids[:, None] == jnp.arange(bucket_count, dtype=jnp.int32)[None, :]
    first_off = jnp.min(jnp.where(bucket_hit, offsets[:, None], piece_rows), axis=0)
    counts = jnp.sum(bucket_hit.astype(jnp.int32), axis=0)
    slot_first = jnp.sum(jnp.where(bucket_hit, first_off[None, :], 0), axis=1)
    rows_at = piece_ids * capacity + offsets - slot_first
    rows_at = jnp.where(is_valid, rows_at, bucket_count * capacity)
    slot_ids = jnp.arange(slot_count, dtype=jnp.int32)
    slot_req = slot_ids // slots_here
    slot_far = (far - slot_req // near_count) % far_count
    slot_near = (near - slot_req % near_count) % near_count
    slot_place = (slot_far * near_count + slot_near) * slots_here + slot_ids % slots_here
    sources = (
        jnp.zeros((bucket_count * capacity,), jnp.int32).at[rows_at].set(slot_place, mode="drop")
    )

    gathered = []
    for s in range(far_count):
        first = merged if s == 0 else shift_far(merged, s)
        gathered += [first] + [shift_near(first, t) for t in range(1, near_count)]
    products = jnp.concatenate(
        [jnp.dot(g, weight_cols, preferred_element_type=jnp.float32).astype(jnp.bfloat16) for g in gathered], axis=0
    )
    picked = jnp.take(products, sources, axis=0)
    out_width = picked.shape[1]
    arrived = lax.all_to_all(
        picked.reshape(bucket_count, capacity, out_width), ("req", "mlp"), split_axis=0, concat_axis=0, tiled=True
    )
    arrived = arrived.reshape(req_count, mlp_count, capacity, out_width).astype(jnp.float32).sum(axis=1)
    arrived = arrived.astype(jnp.bfloat16).transpose(1, 0, 2).reshape(capacity, req_count * out_width)

    bucket_here = req_index * mlp_count + mlp_index
    start_here = first_off[bucket_here]
    count_here = counts[bucket_here]
    window = jnp.minimum(start_here, piece_rows - capacity)
    ranks = jnp.arange(capacity, dtype=jnp.int32) + window - start_here
    inside = (ranks >= 0) & (ranks < count_here)
    image_rows = jnp.take(arrived, jnp.clip(ranks, 0, capacity - 1), axis=0)
    old_rows = lax.dynamic_slice_in_dim(text_rows, window, capacity, axis=0)
    new_rows = jnp.where(inside[:, None], image_rows, old_rows)
    streams = lax.dynamic_update_slice_in_dim(text_rows, new_rows, window, axis=0)
    return (patch_out, streams)


def solution(mesh):
    return jax.shard_map(
        shards,
        mesh=mesh,
        in_specs=(
            P("req", None),
            P(),
            P(),
            P(None, ("req", "mlp")),
            P(None, ("req", "mlp")),
            P(None, ("req", "mlp")),
            P(),
            P(None, "mlp", "req"),
            P(("req", "mlp"), None),
            P(),
        ),
        out_specs=(P("req", "mlp"), P(("req", "mlp"), None)),
        check_vma=False,
    )
```

```python
import jax
import jax.numpy as jnp
from jax import lax
from jax.sharding import PartitionSpec as P


def layer_norm(values, norm_gain, norm_bias):
    row_mean = jnp.mean(values, axis=-1, keepdims=True)
    centred = values - row_mean
    variance = jnp.mean(centred * centred, axis=-1, keepdims=True)
    return centred * lax.rsqrt(variance + 1e-06) * norm_gain + norm_bias


def shards(
    patches,
    norm_gain,
    norm_bias,
    gate_weight,
    up_weight,
    down_weight,
    layer_scale,
    projection,
    text_rows,
    destination,
):
    req_count = lax.axis_size("req")
    mlp_count = lax.axis_size("mlp")
    req_index = lax.axis_index("req")
    mlp_index = lax.axis_index("mlp")
    far_count = 4
    near_count = req_count // far_count
    pair_count = mlp_count // 2
    far, near = req_index // near_count, req_index % near_count
    pair, core = mlp_index // 2, mlp_index % 2

    def swap_far(x, k):
        perm = [
            (f * near_count + n, (f ^ k) * near_count + n) for f in range(far_count) for n in range(near_count)
        ]
        return lax.ppermute(x, "req", perm)

    def shift_near(x, s):
        perm = [
            (f * near_count + n, f * near_count + (n + s) % near_count)
            for f in range(far_count)
            for n in range(near_count)
        ]
        return lax.ppermute(x, "req", perm)

    def shift_pair(x, s):
        perm = [(p * 2 + c, ((p + s) % pair_count) * 2 + c) for p in range(pair_count) for c in range(2)]
        return lax.ppermute(x, "mlp", perm)

    def swap_core(x):
        return lax.ppermute(x, "mlp", [(m, m ^ 1) for m in range(mlp_count)])

    rows_here, model_width = patches.shape
    feat_width = model_width // mlp_count

    def quarter_at(t, d, sign):
        other = (pair + sign * t) % pair_count
        return (other * 2 + (core + d) % 2) * feat_width

    def relative(x, axis, sign, which):
        return jnp.concatenate(
            [lax.dynamic_slice_in_dim(x, quarter_at(t, d, sign), feat_width, axis=axis) for t, d in which], axis=axis
        )

    kept = [(t, 0) for t in range(pair_count)]
    sent = [(t, 1) for t in range(pair_count)]

    weights = jnp.concatenate([gate_weight, up_weight, down_weight], axis=1)
    from_near = [shift_near(weights, s) for s in range(1, near_count)]
    units = gate_weight.shape[1]

    inputs = patches.astype(jnp.float32)
    normed = layer_norm(inputs, norm_gain, norm_bias).astype(jnp.bfloat16)
    own_quarter = lax.dynamic_slice_in_dim(normed, mlp_index * feat_width, feat_width, axis=1)

    quarters = {1: swap_far(own_quarter, 1), 2: swap_far(own_quarter, 2)}
    quarters[1], text_rows = lax.optimization_barrier((quarters[1], text_rows))
    quarters[3] = swap_far(quarters[2], 1)
    halves = {0: (relative(normed, 1, -1, kept), relative(normed, 1, -1, sent))}
    for k in (1, 2, 3):
        first = quarters[k]
        column = jnp.concatenate([first] + [shift_pair(first, t) for t in range(1, pair_count)], axis=1)
        halves[k] = (column, swap_core(column))

    def with_near(index):
        cut = slice(index * units, (index + 1) * units)
        return jnp.concatenate([w[:, cut] for w in [weights] + from_near], axis=1)

    gate_full, up_full, down_full = with_near(0), with_near(1), with_near(2)
    gate_rel = [relative(gate_full, 0, -1, which) for which in (kept, sent)]
    up_rel = [relative(up_full, 0, -1, which) for which in (kept, sent)]
    down_kept = relative(down_full, 0, 1, kept)
    down_sent = relative(down_full, 0, 1, sent)

    def dot(a, w):
        return jnp.dot(a, w, preferred_element_type=jnp.float32)

    def dot_t(a, w):
        return lax.dot_general(a, w, (((1,), (1,)), ((), ())), preferred_element_type=jnp.float32)

    hiddens, from_core, after = {}, {}, None
    for k in (0, 1, 2, 3):
        here, there = halves[k]
        if after is not None:
            here, there, _ = lax.optimization_barrier((here, there, after))
        if k >= 2:
            here, there, from_core[k - 2] = lax.optimization_barrier((here, there, from_core[k - 2]))
        gate_act = dot(here, gate_rel[0]) + dot(there, gate_rel[1])
        up_act = dot(here, up_rel[0]) + dot(there, up_rel[1])
        hiddens[k] = (jax.nn.silu(gate_act) * up_act).astype(jnp.bfloat16)
        after = dot_t(hiddens[k], down_sent).astype(jnp.bfloat16)
        from_core[k] = swap_core(after)

    def over_mlp(k):
        of_core = dot_t(hiddens[k], down_kept) + from_core[k].astype(jnp.float32)
        mine = of_core[:, :feat_width]
        for t in range(1, pair_count):
            part = of_core[:, t * feat_width : (t + 1) * feat_width].astype(jnp.bfloat16)
            mine = mine + shift_pair(part, t).astype(jnp.float32)
        return mine

    def sent_far(x, k):
        return swap_far(x.astype(jnp.bfloat16), k).astype(jnp.float32)

    total = over_mlp(0)
    farthest = sent_far(over_mlp(3), 1)
    total = total + sent_far(over_mlp(2) + farthest, 2)
    total = total + sent_far(over_mlp(1), 1)

    scale_here = lax.dynamic_slice_in_dim(layer_scale, mlp_index * feat_width, feat_width)
    own_inputs = lax.dynamic_slice_in_dim(patches, mlp_index * feat_width, feat_width, axis=1).astype(jnp.float32)
    patch_out = (own_inputs + scale_here * total).astype(jnp.bfloat16)

    merged = patch_out.reshape(rows_here // 4, 4 * feat_width)
    weight_cols = projection.reshape(4 * feat_width, projection.shape[2])
    slots_here = rows_here // 4
    piece_rows = text_rows.shape[0]
    slot_count = destination.shape[0]
    bucket_count = req_count * mlp_count
    capacity = slot_count // bucket_count
    is_valid = destination >= 0
    piece_ids = jnp.where(is_valid, destination // piece_rows, -1)
    offsets = destination % piece_rows
    bucket_hit = piece_ids[:, None] == jnp.arange(bucket_count, dtype=jnp.int32)[None, :]
    first_off = jnp.min(jnp.where(bucket_hit, offsets[:, None], piece_rows), axis=0)
    counts = jnp.sum(bucket_hit.astype(jnp.int32), axis=0)
    slot_first = jnp.sum(jnp.where(bucket_hit, first_off[None, :], 0), axis=1)
    piece_req, piece_mlp = piece_ids // mlp_count, piece_ids % mlp_count
    rel_core = (piece_mlp % 2 - core) % 2
    rel_pair = (piece_mlp // 2 - pair) % pair_count
    rel_piece = (rel_core * pair_count + rel_pair) * req_count + piece_req
    rows_at = rel_piece * capacity + offsets - slot_first
    rows_at = jnp.where(is_valid, rows_at, bucket_count * capacity)
    slot_ids = jnp.arange(slot_count, dtype=jnp.int32)
    slot_req = slot_ids // slots_here
    slot_far = jnp.bitwise_xor(far, slot_req // near_count)
    slot_near = (near - slot_req % near_count) % near_count
    slot_place = (slot_far * near_count + slot_near) * slots_here + slot_ids % slots_here
    sources = (
        jnp.zeros((bucket_count * capacity,), jnp.int32).at[rows_at].set(slot_place, mode="drop")
    )

    firsts = {0: merged, 1: swap_far(merged, 1), 2: swap_far(merged, 2)}
    firsts[3] = swap_far(firsts[2], 1)
    gathered = []
    for k in range(far_count):
        gathered += [firsts[k]] + [shift_near(firsts[k], t) for t in range(1, near_count)]
    products = jnp.concatenate([dot(g, weight_cols).astype(jnp.bfloat16) for g in gathered], axis=0)
    picked = jnp.take(products, sources, axis=0)
    out_width = picked.shape[1]
    half = picked.shape[0] // 2
    core_sum = picked[:half].astype(jnp.float32) + swap_core(picked[half:]).astype(jnp.float32)
    core_sum = core_sum.reshape(pair_count, req_count * capacity, out_width)
    summed = core_sum[0]
    for t in range(1, pair_count):
        summed = summed + shift_pair(core_sum[t].astype(jnp.bfloat16), t).astype(jnp.float32)
    arrived = lax.all_to_all(
        summed.astype(jnp.bfloat16), "req", split_axis=0, concat_axis=1, tiled=True
    )

    bucket_here = req_index * mlp_count + mlp_index
    start_here = first_off[bucket_here]
    count_here = counts[bucket_here]
    window = jnp.minimum(start_here, piece_rows - capacity)
    ranks = jnp.arange(capacity, dtype=jnp.int32) + window - start_here
    inside = (ranks >= 0) & (ranks < count_here)
    image_rows = jnp.take(arrived, jnp.clip(ranks, 0, capacity - 1), axis=0)
    old_rows = lax.dynamic_slice_in_dim(text_rows, window, capacity, axis=0)
    new_rows = jnp.where(inside[:, None], image_rows, old_rows)
    streams = lax.dynamic_update_slice_in_dim(text_rows, new_rows, window, axis=0)
    return (patch_out, streams)


def solution(mesh):
    return jax.shard_map(
        shards,
        mesh=mesh,
        in_specs=(
            P("req", None),
            P(),
            P(),
            P(None, ("req", "mlp")),
            P(None, ("req", "mlp")),
            P(None, ("req", "mlp")),
            P(),
            P(None, "mlp", "req"),
            P(("req", "mlp"), None),
            P(),
        ),
        out_specs=(P("req", "mlp"), P(("req", "mlp"), None)),
        check_vma=False,
    )
```

```python
import jax
import jax.numpy as jnp
from jax import lax
from jax.sharding import PartitionSpec as P


def layer_norm(values, norm_gain, norm_bias):
    row_mean = jnp.mean(values, axis=-1, keepdims=True)
    centred = values - row_mean
    variance = jnp.mean(centred * centred, axis=-1, keepdims=True)
    return centred * lax.rsqrt(variance + 1e-06) * norm_gain + norm_bias


def shards(
    patches,
    norm_gain,
    norm_bias,
    gate_weight,
    up_weight,
    down_weight,
    layer_scale,
    projection,
    text_rows,
    destination,
):
    req_count = lax.axis_size("req")
    mlp_count = lax.axis_size("mlp")
    req_index = lax.axis_index("req")
    mlp_index = lax.axis_index("mlp")
    far_count = 4
    near_count = req_count // far_count
    pair_count = mlp_count // 2
    far, near = req_index // near_count, req_index % near_count
    pair, core = mlp_index // 2, mlp_index % 2

    def swap_far(x, k):
        perm = [
            (f * near_count + n, (f ^ k) * near_count + n) for f in range(far_count) for n in range(near_count)
        ]
        return lax.ppermute(x, "req", perm)

    def shift_near(x, s):
        perm = [
            (f * near_count + n, f * near_count + (n + s) % near_count)
            for f in range(far_count)
            for n in range(near_count)
        ]
        return lax.ppermute(x, "req", perm)

    def shift_pair(x, s):
        perm = [(p * 2 + c, ((p + s) % pair_count) * 2 + c) for p in range(pair_count) for c in range(2)]
        return lax.ppermute(x, "mlp", perm)

    def swap_core(x):
        return lax.ppermute(x, "mlp", [(m, m ^ 1) for m in range(mlp_count)])

    rows_here, model_width = patches.shape
    feat_width = model_width // mlp_count

    def quarter_at(t, d, sign):
        other = (pair + sign * t) % pair_count
        return (other * 2 + (core + d) % 2) * feat_width

    def relative(x, axis, sign, which):
        return jnp.concatenate(
            [lax.dynamic_slice_in_dim(x, quarter_at(t, d, sign), feat_width, axis=axis) for t, d in which], axis=axis
        )

    kept = [(t, 0) for t in range(pair_count)]
    sent = [(t, 1) for t in range(pair_count)]

    weights = jnp.concatenate([gate_weight, up_weight, down_weight], axis=1)
    from_near = [shift_near(weights, s) for s in range(1, near_count)]
    units = gate_weight.shape[1]

    inputs = patches.astype(jnp.float32)
    normed = layer_norm(inputs, norm_gain, norm_bias).astype(jnp.bfloat16)
    own_quarter = lax.dynamic_slice_in_dim(normed, mlp_index * feat_width, feat_width, axis=1)

    quarters = {1: swap_far(own_quarter, 1), 2: swap_far(own_quarter, 2)}
    def moved(first):
        return [first] + [shift_pair(first, t) for t in range(1, pair_count)]

    columns = {1: moved(quarters[1])}
    columns[1], quarters[2] = lax.optimization_barrier((columns[1], quarters[2]))
    quarters[3] = swap_far(quarters[2], 1)
    columns[2] = moved(quarters[2])
    columns[3] = moved(quarters[3])

    def with_near(index):
        cut = slice(index * units, (index + 1) * units)
        return jnp.concatenate([w[:, cut] for w in [weights] + from_near], axis=1)

    gate_full, up_full, down_full = with_near(0), with_near(1), with_near(2)
    gate_rel = [relative(gate_full, 0, -1, which) for which in (kept, sent)]
    up_rel = [relative(up_full, 0, -1, which) for which in (kept, sent)]
    down_kept = relative(down_full, 0, 1, kept)
    down_sent = relative(down_full, 0, 1, sent)

    def dot(a, w):
        return jnp.dot(a, w, preferred_element_type=jnp.float32)

    def dot_t(a, w):
        return lax.dot_general(a, w, (((1,), (1,)), ((), ())), preferred_element_type=jnp.float32)

    hiddens, from_core, afters = {}, {}, {}
    for k in (0, 1, 2, 3):
        if k == 0:
            here, there = relative(normed, 1, -1, kept), relative(normed, 1, -1, sent)
        else:
            if k >= 2:
                columns[k], afters[k - 2] = lax.optimization_barrier((columns[k], afters[k - 2]))
            here = jnp.concatenate(columns[k], axis=1)
            there = swap_core(here)
            here, there, afters[k - 1] = lax.optimization_barrier((here, there, afters[k - 1]))
        if k >= 2:
            here, there, from_core[k - 2] = lax.optimization_barrier((here, there, from_core[k - 2]))
        gate_act = dot(here, gate_rel[0]) + dot(there, gate_rel[1])
        up_act = dot(here, up_rel[0]) + dot(there, up_rel[1])
        hiddens[k] = (jax.nn.silu(gate_act) * up_act).astype(jnp.bfloat16)
        afters[k] = dot_t(hiddens[k], down_sent).astype(jnp.bfloat16)
        from_core[k] = swap_core(afters[k])

    def over_core(k):
        return dot_t(hiddens[k], down_kept) + from_core[k].astype(jnp.float32)

    def over_pair(of_core):
        mine = of_core[:, :feat_width]
        for t in range(1, pair_count):
            part = of_core[:, t * feat_width : (t + 1) * feat_width].astype(jnp.bfloat16)
            mine = mine + shift_pair(part, t).astype(jnp.float32)
        return mine

    def sent_far(x, k):
        return swap_far(x.astype(jnp.bfloat16), k).astype(jnp.float32)

    total = over_pair(over_core(0))
    total, from_core[3] = lax.optimization_barrier((total, from_core[3]))
    third = over_core(3)
    third, from_core[2] = lax.optimization_barrier((third, from_core[2]))
    second = over_core(2)
    third = over_pair(third).astype(jnp.bfloat16)
    third, from_core[1] = lax.optimization_barrier((third, from_core[1]))
    farthest = sent_far(third, 1)
    first = over_core(1)
    total = total + sent_far(over_pair(second) + farthest, 2)
    total = total + sent_far(over_pair(first), 1)

    scale_here = lax.dynamic_slice_in_dim(layer_scale, mlp_index * feat_width, feat_width)
    own_inputs = lax.dynamic_slice_in_dim(patches, mlp_index * feat_width, feat_width, axis=1).astype(jnp.float32)
    patch_out = (own_inputs + scale_here * total).astype(jnp.bfloat16)

    merged = patch_out.reshape(rows_here // 4, 4 * feat_width)
    weight_cols = projection.reshape(4 * feat_width, projection.shape[2])
    slots_here = rows_here // 4
    piece_rows = text_rows.shape[0]
    slot_count = destination.shape[0]
    bucket_count = req_count * mlp_count
    capacity = slot_count // bucket_count
    is_valid = destination >= 0
    piece_ids = jnp.where(is_valid, destination // piece_rows, -1)
    offsets = destination % piece_rows
    bucket_hit = piece_ids[:, None] == jnp.arange(bucket_count, dtype=jnp.int32)[None, :]
    first_off = jnp.min(jnp.where(bucket_hit, offsets[:, None], piece_rows), axis=0)
    counts = jnp.sum(bucket_hit.astype(jnp.int32), axis=0)
    slot_first = jnp.sum(jnp.where(bucket_hit, first_off[None, :], 0), axis=1)
    piece_req, piece_mlp = piece_ids // mlp_count, piece_ids % mlp_count
    rel_core = (piece_mlp % 2 - core) % 2
    rel_pair = (piece_mlp // 2 - pair) % pair_count
    rel_piece = (rel_core * pair_count + rel_pair) * req_count + piece_req
    rows_at = rel_piece * capacity + offsets - slot_first
    rows_at = jnp.where(is_valid, rows_at, bucket_count * capacity)
    slot_ids = jnp.arange(slot_count, dtype=jnp.int32)
    slot_req = slot_ids // slots_here
    slot_far = jnp.bitwise_xor(far, slot_req // near_count)
    slot_near = (near - slot_req % near_count) % near_count
    slot_place = (slot_far * near_count + slot_near) * slots_here + slot_ids % slots_here
    sources = (
        jnp.zeros((bucket_count * capacity,), jnp.int32).at[rows_at].set(slot_place, mode="drop")
    )

    def along_near(first):
        return [first] + [shift_near(first, t) for t in range(1, near_count)]

    firsts = {1: swap_far(merged, 1), 2: swap_far(merged, 2)}
    groups = {0: along_near(merged), 1: along_near(firsts[1])}
    groups[1], firsts[2] = lax.optimization_barrier((groups[1], firsts[2]))
    firsts[3] = swap_far(firsts[2], 1)
    groups[2], groups[3] = along_near(firsts[2]), along_near(firsts[3])
    gathered = groups[0] + groups[1] + groups[2] + groups[3]
    products = jnp.concatenate([dot(g, weight_cols).astype(jnp.bfloat16) for g in gathered], axis=0)
    picked = jnp.take(products, sources, axis=0)
    out_width = picked.shape[1]
    half = picked.shape[0] // 2
    core_sum = picked[:half].astype(jnp.float32) + swap_core(picked[half:]).astype(jnp.float32)
    core_sum = core_sum.reshape(pair_count, req_count * capacity, out_width)
    summed = core_sum[0]
    for t in range(1, pair_count):
        summed = summed + shift_pair(core_sum[t].astype(jnp.bfloat16), t).astype(jnp.float32)
    arrived = lax.all_to_all(
        summed.astype(jnp.bfloat16), "req", split_axis=0, concat_axis=1, tiled=True
    )

    bucket_here = req_index * mlp_count + mlp_index
    start_here = first_off[bucket_here]
    count_here = counts[bucket_here]
    window = jnp.minimum(start_here, piece_rows - capacity)
    ranks = jnp.arange(capacity, dtype=jnp.int32) + window - start_here
    inside = (ranks >= 0) & (ranks < count_here)
    image_rows = jnp.take(arrived, jnp.clip(ranks, 0, capacity - 1), axis=0)
    old_rows = lax.dynamic_slice_in_dim(text_rows, window, capacity, axis=0)
    new_rows = jnp.where(inside[:, None], image_rows, old_rows)
    streams = lax.dynamic_update_slice_in_dim(text_rows, new_rows, window, axis=0)
    return (patch_out, streams)


def solution(mesh):
    return jax.shard_map(
        shards,
        mesh=mesh,
        in_specs=(
            P("req", None),
            P(),
            P(),
            P(None, ("req", "mlp")),
            P(None, ("req", "mlp")),
            P(None, ("req", "mlp")),
            P(),
            P(None, "mlp", "req"),
            P(("req", "mlp"), None),
            P(),
        ),
        out_specs=(P("req", "mlp"), P(("req", "mlp"), None)),
        check_vma=False,
    )
```
